32 devices in a mesh: pair: 8 (over z, x), virt: 4 (over y, core).
Axes of the slice: x: 2, y: 2, z: 4, core: 2. Of those that a mesh axis runs over, the one named last changes fastest.
Arguments:
- amplitudes: bfloat16 [8192, 8, 1024], P('pair', 'virt'), may hold values from -6 to 6
- tile_mask: int32 [8192, 8], P('pair', 'virt'), may hold values from 0 to 1
- integrals: bfloat16 [8, 1024, 1024], P('virt', 'pair'), may hold values from -0.0625 to 0.0625
- pair_energy: float32 [8192], P(('pair', 'virt')), may hold values from -2 to -0.5
- virt_energy: float32 [1024], replicated, may hold values from 0.5 to 3
Outputs:
- update: bfloat16 [8192, 1024], P(('pair', 'virt'))
The draws below stay inside these ranges and needn't reach their ends.
All inputs are finite; a program needn't handle non-finite values.
Results may differ from the reference program's by a relative error of at most 0.011.
Values may be sent and summed in bfloat16 or wider, within the bound.
No kernel may reach another device: no remote copies, remote signals or barrier semaphores. Data moves between devices by JAX's collectives and lax.ppermute only.
A program may use at most 64 MiB of HBM per device.

```python
import jax
import jax.numpy as jnp
from jax import lax

AB = 1024
CD = 1024
CD_DEV = 2
PAIR_DEV = 1024
NCD = 8
PAIRS = 8192


def draw_tile_mask(key, part):
    level = jax.random.randint(key, (PAIRS, NCD), 0, 4 * PAIRS)
    rising = PAIRS + 3 * jnp.arange(PAIRS, dtype=jnp.int32)[:, None]
    return (level < rising).astype(jnp.int32)


def level_of(stream_key, extent, cuts, smallest, largest):
    factor_of = 1.0
    for dim, parts in cuts:
        draws = jax.random.uniform(jax.random.fold_in(jax.random.fold_in(stream_key, 6), dim), (parts,), jnp.float32, smallest / len(cuts), largest / len(cuts))
        factor_of = factor_of * jnp.repeat(jnp.exp(draws), extent[dim] // parts).reshape((-1,) + (1,) * (len(extent) - 1 - dim))
    return factor_of


def centred(rng, dims, scale, bound, cuts=(), kind=jnp.bfloat16):
    entries = scale * jax.random.normal(rng, dims, jnp.float32)
    if cuts:
        entries = entries * level_of(rng, dims, cuts, -0.22, 0.18)
    return jnp.clip(entries, -bound, bound).astype(kind)


def setup_inputs(seed: int = 0) -> dict:
    arg_keys = jax.random.split(jax.random.key(seed), 6)
    return {
        "amplitudes": centred(arg_keys[0], (PAIRS, NCD, CD), 1.0, 6.0, ((0, 8), (1, 4))),
        "tile_mask": draw_tile_mask(jax.random.fold_in(arg_keys[5], 71), 0),
        "integrals": centred(arg_keys[2], (NCD, CD, AB), (NCD * CD) ** -0.5, 0.0625, ((0, 4), (1, 8))),
        "pair_energy": jnp.clip(-2.0 + 1.5 * jax.random.uniform(arg_keys[3], (PAIRS,), jnp.float32) ** level_of(arg_keys[3], (PAIRS,), ((0, 32),), -0.2, 0.2), -2.0, -0.5),
        "virt_energy": jnp.clip(jax.random.uniform(arg_keys[4], (AB,), jnp.float32, 0.5, 3.0), 0.5, 3.0),
    }


def reference(amplitudes, tile_mask, integrals, pair_energy, virt_energy):
    groups = NCD // CD_DEV
    masked = amplitudes * tile_mask.astype(jnp.bfloat16)[:, :, None]
    blocks = masked.reshape(PAIRS // PAIR_DEV, PAIR_DEV, NCD, CD)
    tiles = integrals.astype(jnp.float32)

    def one_block(block):
        fblock = block.astype(jnp.float32)
        total = jnp.zeros((PAIR_DEV, AB), jnp.float32)
        for group in range(groups):
            lo = group * CD_DEV
            part = jnp.einsum("ptk,tkn->pn", fblock[:, lo:lo + CD_DEV, :], tiles[lo:lo + CD_DEV])
            part = part.astype(jnp.bfloat16)
            part = lax.optimization_barrier(part)
            total = total + part.astype(jnp.float32)
        return total

    ladder = lax.map(one_block, blocks).reshape(PAIRS, AB)
    denom = virt_energy[None, :] - pair_energy[:, None]
    return (ladder / denom).astype(jnp.bfloat16)
```

```python
import functools

import jax
import jax.numpy as jnp
from jax import lax
from jax.experimental import pallas as pl
from jax.experimental.pallas import tpu as pltpu
from jax.sharding import PartitionSpec as P

BF16 = jnp.bfloat16
F32 = jnp.float32


def plain(amplitudes, tile_mask, integrals, pair_energy, virt_energy):
    masked = amplitudes * tile_mask.astype(BF16)[:, :, None]
    partial_value = jnp.einsum(
        "ptk,tkn->pn",
        masked,
        lax.all_gather(integrals, "pair", axis=1, tiled=True),
        preferred_element_type=F32,
    )
    ladder = lax.psum_scatter(partial_value.astype(BF16), "virt", scatter_dimension=0, tiled=True).astype(F32)
    denom = virt_energy[None, :] - pair_energy[:, None]
    return (ladder / denom).astype(BF16)


def line(z_pairs, flip=False):
    return [(a * 2 + x, b * 2 + (1 - x if flip else x)) for a, b in z_pairs for x in range(2)]


Z1 = line([(0, 1), (1, 0), (2, 3), (3, 2)])
Z2 = line([(0, 2), (2, 0), (1, 3), (3, 1)])
ZMID = line([(1, 2), (2, 1)])
ZEND = line([(1, 0), (2, 3)])
XALL = line([(z, z) for z in range(4)], True)
XMID = line([(1, 1), (2, 2)], True)
XEND = line([(0, 0), (3, 3)], True)
CORE = [(0, 1), (1, 0), (2, 3), (3, 2)]
YHOP = [(0, 2), (2, 0), (1, 3), (3, 1)]


def over_pair(value, hops):
    return lax.ppermute(value, "pair", hops)


def over_virt(value, hops):
    return lax.ppermute(value, "virt", hops)


def after(value, *others):
    return lax.optimization_barrier((value,) + others)[0]


def products(places, rows, a, blocks, ends, total=None, finish=False):
    depth, columns = blocks[0].shape if blocks else ends[0][0].shape
    n_blocks = len(blocks) + len(ends)
    row = a.shape[1] // 4
    refs_in = list(blocks) + [e for pair in ends for e in pair]

    def body(places_ref, rows_ref, a_ref, *refs):
        ins = refs[: len(refs_in)]
        rest = refs[len(refs_in):]
        if total is not None:
            acc = rest[0][0]
            rest = rest[1:]
        else:
            acc = jnp.zeros((row, columns), F32)
        for k in range(n_blocks):
            if k < len(blocks):
                block = ins[k][...]
            else:
                e = len(blocks) + 2 * (k - len(blocks))
                block = ins[e][...] + ins[e + 1][...]
            acc += jnp.dot(a_ref[places_ref[k]], block, preferred_element_type=F32)
        if not finish:
            rest[0][0] = acc
            return
        step = pl.program_id(0)

        @pl.when(step < 2)
        def _():
            rest[0][0] = acc.astype(BF16)

        @pl.when(step >= 2)
        def _():
            rest[1][0] = acc

    in_specs = [pl.BlockSpec((a.shape[0], row, depth), lambda i, p, r: (0, r[i], 0))]
    in_specs += [pl.BlockSpec((depth, columns), lambda i, p, r: (0, 0))] * len(refs_in)
    operands = [a] + refs_in
    if total is not None:
        in_specs.append(pl.BlockSpec((1, row, columns), lambda i, p, r: (i, 0, 0)))
        operands.append(total)
    if finish:
        out_specs = [
            pl.BlockSpec((1, row, columns), lambda i, p, r: (jnp.minimum(i, 1), 0, 0)),
            pl.BlockSpec((1, row, columns), lambda i, p, r: (jnp.maximum(i - 2, 0), 0, 0)),
        ]
        out_shape = [
            jax.ShapeDtypeStruct((2, row, columns), BF16),
            jax.ShapeDtypeStruct((2, row, columns), F32),
        ]
    else:
        out_specs = pl.BlockSpec((1, row, columns), lambda i, p, r: (i, 0, 0))
        out_shape = jax.ShapeDtypeStruct((4, row, columns), F32)
    return pl.pallas_call(
        body,
        grid_spec=pltpu.PrefetchScalarGridSpec(
            num_scalar_prefetch=2, grid=(4,), in_specs=in_specs, out_specs=out_specs
        ),
        out_shape=out_shape,
        compiler_params=pltpu.CompilerParams(vmem_limit_bytes=48 * 2**20),
        cost_estimate=pl.CostEstimate(
            flops=2 * a.shape[1] * depth * n_blocks * columns,
            bytes_accessed=2 * a.size + 2 * n_blocks * depth * columns,
            transcendentals=0,
        ),
    )(places, rows, *operands)


def scheduled(cut, amplitudes, tile_mask, integrals, pair_energy, virt_energy):
    pairs, tiles, wide = amplitudes.shape
    depth, columns = integrals.shape[1:]
    pair, virt = lax.axis_index("pair"), lax.axis_index("virt")
    z, x = pair // 2, pair % 2
    y, core = virt // 2, virt % 2
    corner = (z == 0) | (z == 3)

    def ab(v):
        return v.reshape(tiles * depth, v.shape[-1])

    x0 = over_pair(integrals, XALL)
    own_a, own_b = integrals[:, :, :cut], integrals[:, :, cut:]
    p1a = over_pair(own_a, Z1)
    p2a = over_pair(own_a, Z2)

    masked = amplitudes * tile_mask.astype(BF16)[:, :, None]
    a = masked.reshape(pairs, tiles, 8, depth).transpose(2, 0, 1, 3).reshape(8, pairs, tiles * depth)

    x1a = over_pair(p1a, XALL)
    p1b = over_pair(after(own_b, p1a), Z1)
    p3ea = over_pair(p2a, ZEND)
    x2a = over_pair(p2a, XALL)
    p2b = over_pair(after(own_b, p2a), Z2)
    p3ma = over_pair(after(own_a, p1b), ZMID)
    x1b = over_pair(x0[:, :, cut:], Z1)
    x2b = over_pair(p2b, XALL)
    p3eb = over_pair(p2b, ZEND)
    p3mb = over_pair(after(own_b, p2b), ZMID)
    x3ea = over_pair(p3ea, XEND)
    x3ma = over_pair(p3ma, XMID)
    x3eb = over_pair(p3eb, XEND)
    x3mb = over_pair(p3mb, XMID)

    near, far = z ^ 1, z ^ 2
    third = z ^ 3
    zs = jnp.stack([z, z, near, near, far, far, third, third])
    xs = jnp.stack([x, 1 - x] * 4)
    places = (zs * 2 + xs).astype(jnp.int32)
    rows = jnp.stack(
        [2 * (1 - y) + 1 - core, 2 * y + 1 - core, 2 * (1 - y) + core, 2 * y + core]
    ).astype(jnp.int32)

    first = [ab(v) for v in (own_a, x0[:, :, :cut], p1a, x1a, p2a, x2a)]
    send_a, keep_a = products(
        places, rows, a, first, [(ab(p3ma), ab(p3ea)), (ab(x3ma), ab(x3ea))], finish=True
    )
    got_a = over_virt(send_a, CORE)
    there_a = over_virt((keep_a[0] + got_a[0].astype(F32)).astype(BF16), YHOP)

    second = [ab(v) for v in (own_b, x0[:, :, cut:], p1b, x1b, p2b, x2b)]
    total_b = products(places[:7], rows, a, second, [(ab(p3mb), ab(p3eb))])
    send_b, keep_b = products(places[7:], rows, a, [], [(ab(x3mb), ab(x3eb))], total=total_b, finish=True)
    got_b = over_virt(send_b, CORE)
    there_b = over_virt((keep_b[0] + got_b[0].astype(F32)).astype(BF16), YHOP)

    ladder = jnp.concatenate(
        [
            keep_a[1] + got_a[1].astype(F32) + there_a.astype(F32),
            keep_b[1] + got_b[1].astype(F32) + there_b.astype(F32),
        ],
        axis=1,
    )
    denom = virt_energy[None, :] - pair_energy[:, None]
    return (ladder / denom).astype(BF16)


def solution(mesh):
    placed = (
        P("pair", "virt", None),
        P("pair", "virt"),
        P("virt", "pair", None),
        P(("pair", "virt")),
        P(),
    )
    here = mesh.shape["pair"] == 8 and mesh.shape["virt"] == 4
    return jax.shard_map(
        functools.partial(scheduled, 640) if here else plain,
        mesh=mesh,
        in_specs=placed,
        out_specs=P(("pair", "virt"), None),
        check_vma=False,
    )
```

```python
import jax
import jax.numpy as jnp
from jax import lax
from jax.experimental import pallas as pl
from jax.experimental.pallas import tpu as pltpu
from jax.sharding import PartitionSpec as P

BF16 = jnp.bfloat16
F32 = jnp.float32


def plain(amplitudes, tile_mask, integrals, pair_energy, virt_energy):
    masked = amplitudes * tile_mask.astype(BF16)[:, :, None]
    partial_value = jnp.einsum(
        "ptk,tkn->pn",
        masked,
        lax.all_gather(integrals, "pair", axis=1, tiled=True),
        preferred_element_type=F32,
    )
    ladder = lax.psum_scatter(partial_value.astype(BF16), "virt", scatter_dimension=0, tiled=True).astype(F32)
    denom = virt_energy[None, :] - pair_energy[:, None]
    return (ladder / denom).astype(BF16)


RING = [0, 2, 4, 6, 7, 5, 3, 1]
EVEN = [(RING[i], RING[i ^ 1]) for i in range(8)]
ODD = [(RING[i], RING[(i + 2 * (i % 2) - 1) % 8]) for i in range(8)]
CORE = [(0, 1), (1, 0), (2, 3), (3, 2)]
YHOP = [(0, 2), (2, 0), (1, 3), (3, 1)]


def over_pair(value, hops):
    return lax.ppermute(value, "pair", hops)


def over_virt(value, hops):
    return lax.ppermute(value, "virt", hops)


def tie(*values):
    return lax.optimization_barrier(values)


def products(table, slots, a, blocks, span, total=None, finish=False):
    blocks = [b if isinstance(b, list) else [b] for b in blocks]
    flat = [v for b in blocks for v in b]
    tiles, depth = flat[0].shape[:2]
    lo, hi = span
    columns = hi - lo
    row = a.shape[1] // 4

    def body(table_ref, a_ref, *refs):
        ins, outs = list(refs[: len(flat)]), refs[len(flat):]
        if total is not None:
            total_ref, outs = outs[0], outs[1:]
        groups = [[ins.pop(0) for _ in b] for b in blocks]

        def sums(i):
            here = pl.ds(pl.multiple_of(table_ref[8 + i] * row, row), row)
            left, right = [], []
            for slot, group in zip(slots, groups):
                cols = pl.ds(pl.multiple_of(table_ref[slot] * depth, depth), depth)
                left += [a_ref[t, here, cols] for t in range(tiles)]
                pieces = [r[:, :, lo:hi] if r.shape[2] > columns else r[...] for r in group]
                block = pieces[0] if len(pieces) == 1 else jnp.concatenate(pieces, axis=2)
                right.append(block.reshape(tiles * depth, columns))
            acc = jnp.dot(
                jnp.concatenate(left, axis=1), jnp.concatenate(right, axis=0), preferred_element_type=F32
            )
            return acc if total is None else acc + total_ref[i, :, lo:hi]

        if finish:

            @pl.loop(0, 2)
            def _(i):
                outs[0][i] = sums(i).astype(BF16)

            @pl.loop(2, 4)
            def _(i):
                outs[1][i - 2] = sums(i)

        else:

            @pl.loop(0, 4)
            def _(i):
                outs[0][i] = sums(i)

    vmem = pl.BlockSpec(memory_space=pltpu.VMEM)
    smem = pl.BlockSpec(memory_space=pltpu.SMEM)
    operands = [a] + flat + ([] if total is None else [total])
    if finish:
        out_shape = [
            jax.ShapeDtypeStruct((2, row, columns), BF16),
            jax.ShapeDtypeStruct((2, row, columns), F32),
        ]
    else:
        out_shape = [jax.ShapeDtypeStruct((4, row, columns), F32)]
    out = pl.pallas_call(
        body,
        in_specs=[smem] + [vmem] * len(operands),
        out_specs=[vmem] * len(out_shape),
        out_shape=out_shape,
        compiler_params=pltpu.CompilerParams(vmem_limit_bytes=20 * 2**20),
        cost_estimate=pl.CostEstimate(
            flops=2 * a.shape[1] * tiles * depth * len(blocks) * columns,
            bytes_accessed=2 * a.size + 2 * len(flat) * tiles * depth * columns,
            transcendentals=0,
        ),
    )(table, *operands)
    return out if finish else out[0]


def device_table():
    even, odd = dict(EVEN), dict(ODD)
    places = []
    for p in range(8):
        slots = [p, even[p], odd[p], odd[even[p]], even[odd[p]], even[odd[even[p]]], odd[even[odd[p]]]]
        places.append(slots + [sum(range(8)) - sum(slots)])
    every = [places[p] + [v ^ s for s in (3, 1, 2, 0)] for p in range(8) for v in range(4)]
    me = lax.axis_index(("pair", "virt"))
    return lax.dynamic_index_in_dim(jnp.array(every, jnp.int32), me, keepdims=False)


def scheduled(amplitudes, tile_mask, integrals, pair_energy, virt_energy):
    table = device_table()
    columns = integrals.shape[2]
    half, quarter = columns // 2, columns // 4
    span_a, span_b = (0, half), (half, columns)

    def part(v, span):
        return v[:, :, span[0] : span[1]]

    e1, o1 = over_pair(integrals, EVEN), over_pair(integrals, ODD)
    masked = amplitudes * tile_mask.astype(BF16)[:, :, None]
    a = masked.transpose(1, 0, 2)
    e1, a, table = tie(e1, a, table)

    def second(span):
        return over_pair(part(o1, span), EVEN), over_pair(part(e1, span), ODD)

    def third(e2, o2):
        return over_pair(o2, EVEN), over_pair(e2, ODD)

    def fourth(e3, o3):
        return [over_pair(o3[:, :, :quarter], EVEN), over_pair(e3[:, :, quarter:], ODD)]

    e2a, o2a = second(span_a)
    e2b, o2b = second(span_b)
    e3a, o3a = third(e2a, o2a)
    e3b, o3b = third(e2b, o2b)
    total = products(table, [0, 1, 2], a, [integrals, e1, o1], (0, columns))
    e3a, o3a, e2b, o2b, total = tie(e3a, o3a, e2b, o2b, total)
    lasta = fourth(e3a, o3a)
    lasta[0], lasta[1], e3b, o3b = tie(lasta[0], lasta[1], e3b, o3b)
    lastb = fourth(e3b, o3b)

    def shared(blocks, span):
        return products(table, [3, 4, 5, 6, 7], a, blocks, span, total=total, finish=True)

    send_a, keep_a = shared([e2a, o2a, e3a, o3a, lasta], span_a)
    got_a = over_virt(send_a, CORE)
    send_b, keep_b = shared([e2b, o2b, e3b, o3b, lastb], span_b)
    got_a, send_b = tie(got_a, send_b)
    there_a = over_virt((keep_a[0] + got_a[0].astype(F32)).astype(BF16), YHOP)
    got_b = over_virt(send_b, CORE)
    there_b = over_virt((keep_b[0] + got_b[0].astype(F32)).astype(BF16), YHOP)

    ladder = jnp.concatenate(
        [
            keep_a[1] + got_a[1].astype(F32) + there_a.astype(F32),
            keep_b[1] + got_b[1].astype(F32) + there_b.astype(F32),
        ],
        axis=1,
    )
    denom = virt_energy[None, :] - pair_energy[:, None]
    return (ladder / denom).astype(BF16)


def solution(mesh):
    placed = (
        P("pair", "virt", None),
        P("pair", "virt"),
        P("virt", "pair", None),
        P(("pair", "virt")),
        P(),
    )
    here = mesh.shape["pair"] == 8 and mesh.shape["virt"] == 4
    return jax.shard_map(
        scheduled if here else plain,
        mesh=mesh,
        in_specs=placed,
        out_specs=P(("pair", "virt"), None),
        check_vma=False,
    )
```

```python
import functools

import jax
import jax.numpy as jnp
from jax import lax
from jax.experimental import pallas as pl
from jax.experimental.pallas import tpu as pltpu
from jax.sharding import PartitionSpec as P

BF16 = jnp.bfloat16
F32 = jnp.float32


def plain(amplitudes, tile_mask, integrals, pair_energy, virt_energy):
    masked = amplitudes * tile_mask.astype(BF16)[:, :, None]
    partial_value = jnp.einsum(
        "ptk,tkn->pn",
        masked,
        lax.all_gather(integrals, "pair", axis=1, tiled=True),
        preferred_element_type=F32,
    )
    ladder = lax.psum_scatter(partial_value.astype(BF16), "virt", scatter_dimension=0, tiled=True).astype(F32)
    denom = virt_energy[None, :] - pair_energy[:, None]
    return (ladder / denom).astype(BF16)


RING = [0, 2, 4, 6, 7, 5, 3, 1]
EVEN = [(RING[i], RING[i ^ 1]) for i in range(8)]
ODD = [(RING[i], RING[(i + 2 * (i % 2) - 1) % 8]) for i in range(8)]
CORE = [(0, 1), (1, 0), (2, 3), (3, 2)]
YHOP = [(0, 2), (2, 0), (1, 3), (3, 1)]


def over_pair(value, hops):
    return lax.ppermute(value, "pair", hops)


def over_virt(value, hops):
    return lax.ppermute(value, "virt", hops)


def tie(*values):
    return lax.optimization_barrier(values)


def products(table, slots, a, blocks, span, total=None, finish=False, weight=1):
    blocks = [b if isinstance(b, list) else [b] for b in blocks]
    flat = [v for b in blocks for v in b]
    tiles, depth = flat[0].shape[:2]
    lo, hi = span
    columns = hi - lo
    row = a.shape[1] // 4

    def body(table_ref, a_ref, *refs):
        ins, outs = list(refs[: len(flat)]), refs[len(flat):]
        if total is not None:
            total_ref, outs = outs[0], outs[1:]
        groups = [[ins.pop(0) for _ in b] for b in blocks]
        for i in range(4):
            here = pl.ds(pl.multiple_of(table_ref[8 + i] * row, row), row)
            left, right = [], []
            for slot, group in zip(slots, groups):
                cols = pl.ds(pl.multiple_of(table_ref[slot] * depth, depth), depth)
                left += [a_ref[t, here, cols] for t in range(tiles)]
                pieces = [r[:, :, lo:hi] if len(group) == 1 and r.shape[2] > columns else r[...] for r in group]
                block = pieces[0] if len(pieces) == 1 else jnp.concatenate(pieces, axis=2)
                right.append(block.reshape(tiles * depth, columns))
            acc = jnp.dot(
                jnp.concatenate(left, axis=1), jnp.concatenate(right, axis=0), preferred_element_type=F32
            )
            if total is not None:
                acc += total_ref[i, :, lo:hi] if total.shape[2] > columns else total_ref[i]
            if not finish:
                outs[0][i] = acc
            else:
                outs[i][...] = acc.astype(outs[i].dtype)

    vmem = pl.BlockSpec(memory_space=pltpu.VMEM)
    smem = pl.BlockSpec(memory_space=pltpu.SMEM)
    operands = [a] + flat + ([] if total is None else [total])
    if finish:
        out_shape = [jax.ShapeDtypeStruct((row, columns), t) for t in (BF16, BF16, F32, F32)]
    else:
        out_shape = [jax.ShapeDtypeStruct((4, row, columns), F32)]
    out = pl.pallas_call(
        body,
        in_specs=[smem] + [vmem] * len(operands),
        out_specs=[vmem] * len(out_shape),
        out_shape=out_shape,
        compiler_params=pltpu.CompilerParams(vmem_limit_bytes=20 * 2**20),
        cost_estimate=pl.CostEstimate(
            flops=weight * 2 * a.shape[1] * tiles * depth * len(blocks) * columns,
            bytes_accessed=2 * a.size + 2 * len(flat) * tiles * depth * columns,
            transcendentals=0,
        ),
    )(table, *operands)
    return out if finish else out[0]


def device_table():
    even, odd = dict(EVEN), dict(ODD)
    places = []
    for p in range(8):
        slots = [p, even[p], odd[p], odd[even[p]], even[odd[p]], even[odd[even[p]]], odd[even[odd[p]]]]
        places.append(slots + [sum(range(8)) - sum(slots)])
    every = [places[p] + [v ^ s for s in (3, 1, 2, 0)] for p in range(8) for v in range(4)]
    me = lax.axis_index(("pair", "virt"))
    return lax.dynamic_index_in_dim(jnp.array(every, jnp.int32), me, keepdims=False)


def scheduled(cut, amplitudes, tile_mask, integrals, pair_energy, virt_energy):
    table = device_table()
    columns = integrals.shape[2]
    span_a, span_b = (0, cut), (cut, columns)

    def part(v, span):
        return v[:, :, span[0] : span[1]]

    e1, o1 = over_pair(integrals, EVEN), over_pair(integrals, ODD)
    masked = amplitudes * tile_mask.astype(BF16)[:, :, None]
    a = masked.transpose(1, 0, 2)
    e1, a, table = tie(e1, a, table)

    def second(span):
        return over_pair(part(o1, span), EVEN), over_pair(part(e1, span), ODD)

    def third(e2, o2):
        return over_pair(o2, EVEN), over_pair(e2, ODD)

    def fourth(e3, o3):
        middle = e3.shape[2] // 2
        return [over_pair(o3[:, :, :middle], EVEN), over_pair(e3[:, :, middle:], ODD)]

    e2a, o2a = second(span_a)
    e2b, o2b = second(span_b)
    total = products(table, [0, 1, 2], a, [integrals, e1, o1], (0, columns))
    o2a, e2a, total = tie(o2a, e2a, total)
    e3a, o3a = third(e2a, o2a)
    e3b, o3b = third(e2b, o2b)
    total = products(table, [3, 4], a, [[e2a, e2b], [o2a, o2b]], (0, columns), total=total)
    e3a, o3a, total = tie(e3a, o3a, total)
    last_a = fourth(e3a, o3a)

    total_a = products(table, [5, 6], a, [e3a, o3a], span_a, total=total, weight=20)
    e3b, o3b, total_a = tie(e3b, o3b, total_a)
    last_b = fourth(e3b, o3b)
    total_b = products(table, [5, 6], a, [e3b, o3b], span_b, total=total)
    there_a, here_a, keep_there_a, keep_here_a = products(
        table, [7], a, [last_a], span_a, total=total_a, finish=True
    )
    got_there_a, got_here_a = over_virt(there_a, CORE), over_virt(here_a, CORE)
    there_b, here_b, keep_there_b, keep_here_b = products(
        table, [7], a, [last_b], span_b, total=total_b, finish=True, weight=20
    )
    got_there_a, there_b = tie(got_there_a, there_b)
    from_y_a = over_virt((keep_there_a + got_there_a.astype(F32)).astype(BF16), YHOP)
    got_there_b, got_here_b = over_virt(there_b, CORE), over_virt(here_b, CORE)
    from_y_b = over_virt((keep_there_b + got_there_b.astype(F32)).astype(BF16), YHOP)

    ladder = jnp.concatenate(
        [
            keep_here_a + got_here_a.astype(F32) + from_y_a.astype(F32),
            keep_here_b + got_here_b.astype(F32) + from_y_b.astype(F32),
        ],
        axis=1,
    )
    denom = virt_energy[None, :] - pair_energy[:, None]
    return (ladder / denom).astype(BF16)


def solution(mesh):
    placed = (
        P("pair", "virt", None),
        P("pair", "virt"),
        P("virt", "pair", None),
        P(("pair", "virt")),
        P(),
    )
    here = mesh.shape["pair"] == 8 and mesh.shape["virt"] == 4
    return jax.shard_map(
        functools.partial(scheduled, 512) if here else plain,
        mesh=mesh,
        in_specs=placed,
        out_specs=P(("pair", "virt"), None),
        check_vma=False,
    )
```

```python
import jax
import jax.numpy as jnp
from jax import lax
from jax.experimental import pallas as pl
from jax.experimental.pallas import tpu as pltpu
from jax.sharding import PartitionSpec as P

BF16 = jnp.bfloat16
F32 = jnp.float32


def plain(amplitudes, tile_mask, integrals, pair_energy, virt_energy):
    masked = amplitudes * tile_mask.astype(BF16)[:, :, None]
    partial_value = jnp.einsum(
        "ptk,tkn->pn",
        masked,
        lax.all_gather(integrals, "pair", axis=1, tiled=True),
        preferred_element_type=F32,
    )
    ladder = lax.psum_scatter(partial_value.astype(BF16), "virt", scatter_dimension=0, tiled=True).astype(F32)
    denom = virt_energy[None, :] - pair_energy[:, None]
    return (ladder / denom).astype(BF16)


RING = [0, 2, 4, 6, 7, 5, 3, 1]
EVEN = [(RING[i], RING[i ^ 1]) for i in range(8)]
ODD = [(RING[i], RING[(i + 2 * (i % 2) - 1) % 8]) for i in range(8)]
CORE = [(0, 1), (1, 0), (2, 3), (3, 2)]
YHOP = [(0, 2), (2, 0), (1, 3), (3, 1)]


def over_pair(value, hops):
    return lax.ppermute(value, "pair", hops)


def over_virt(value, hops):
    return lax.ppermute(value, "virt", hops)


def arranged(amplitudes, tile_mask):
    pairs, tiles, wide = amplitudes.shape
    rows = 128

    def body(amplitudes_ref, mask_ref, out_ref):
        apart = lax.broadcasted_iota(jnp.int32, (rows, rows * tiles), 1) - tiles * lax.broadcasted_iota(
            jnp.int32, (rows, rows * tiles), 0
        )
        for at in range(0, pairs, rows):
            here = pl.ds(at, rows)
            mixed = amplitudes_ref[here].reshape(rows * tiles, wide)
            mask = jnp.transpose(jnp.concatenate([mask_ref[:, here].astype(F32)] * (8 // tiles), axis=0))
            for t in range(tiles):
                chosen = jnp.where(apart == t, mask[:, t : t + 1], 0.0).astype(BF16)
                out_ref[t, here] = jnp.dot(chosen, mixed, preferred_element_type=F32).astype(BF16)

    vmem = pl.BlockSpec(memory_space=pltpu.VMEM)
    return pl.pallas_call(
        body,
        in_specs=[vmem, vmem],
        out_specs=vmem,
        out_shape=jax.ShapeDtypeStruct((tiles, pairs, wide), BF16),
        compiler_params=pltpu.CompilerParams(vmem_limit_bytes=12 * 2**20),
        cost_estimate=pl.CostEstimate(
            flops=4 * rows * tiles * amplitudes.size, bytes_accessed=4 * amplitudes.size, transcendentals=0
        ),
    )(amplitudes, tile_mask.T)


def added(kept, got):
    def body(kept_ref, got_ref, out_ref):
        out_ref[...] = (kept_ref[...] + got_ref[...].astype(F32)).astype(BF16)

    vmem = pl.BlockSpec(memory_space=pltpu.VMEM)
    return pl.pallas_call(
        body,
        in_specs=[vmem, vmem],
        out_specs=vmem,
        out_shape=jax.ShapeDtypeStruct(kept.shape, BF16),
        compiler_params=pltpu.CompilerParams(vmem_limit_bytes=4 * 2**20),
        cost_estimate=pl.CostEstimate(flops=0, bytes_accessed=0, transcendentals=0),
    )(kept, got)


def tie(*values):
    return lax.optimization_barrier(values)


def products(table, slots, a, blocks, span, total=None, finish=False, weight=1):
    blocks = [b if isinstance(b, list) else [b] for b in blocks]
    flat = [v for b in blocks for v in b]
    tiles, depth = flat[0].shape[:2]
    lo, hi = span
    columns = hi - lo
    row = a.shape[1] // 4

    def body(table_ref, a_ref, *refs):
        ins, outs = list(refs[: len(flat)]), refs[len(flat):]
        if total is not None:
            total_ref, outs = outs[0], outs[1:]
        groups = [[ins.pop(0) for _ in b] for b in blocks]
        for i in range(4):
            here = pl.ds(pl.multiple_of(table_ref[8 + i] * row, row), row)
            left, right = [], []
            for slot, group in zip(slots, groups):
                cols = pl.ds(pl.multiple_of(table_ref[slot] * depth, depth), depth)
                left += [a_ref[t, here, cols] for t in range(tiles)]
                sides = [r[:, :, lo:hi] if len(group) == 1 and r.shape[2] > columns else r[...] for r in group]
                block = sides[0] if len(sides) == 1 else jnp.concatenate(sides, axis=2)
                right.append(block.reshape(tiles * depth, columns))
            acc = jnp.dot(
                jnp.concatenate(left, axis=1), jnp.concatenate(right, axis=0), preferred_element_type=F32
            )
            if total is not None:
                acc += total_ref[i, :, lo:hi] if total.shape[2] > columns else total_ref[i]
            if finish:
                outs[i - 1][...] = acc.astype(outs[i - 1].dtype)
            else:
                outs[0][i] = acc

    vmem = pl.BlockSpec(memory_space=pltpu.VMEM)
    smem = pl.BlockSpec(memory_space=pltpu.SMEM)
    operands = [a] + flat + ([] if total is None else [total])
    if finish:
        out_shape = [jax.ShapeDtypeStruct((row, columns), t) for t in (BF16, F32, F32, BF16)]
    else:
        out_shape = [jax.ShapeDtypeStruct((4, row, columns), F32)]
    out = pl.pallas_call(
        body,
        in_specs=[smem] + [vmem] * len(operands),
        out_specs=[vmem] * len(out_shape),
        out_shape=out_shape,
        compiler_params=pltpu.CompilerParams(vmem_limit_bytes=20 * 2**20),
        cost_estimate=pl.CostEstimate(
            flops=weight * 2 * a.shape[1] * tiles * depth * len(blocks) * columns,
            bytes_accessed=min(weight, 1) * (2 * a.size + 2 * len(flat) * tiles * depth * columns),
            transcendentals=0,
        ),
    )(table, *operands)
    return out if finish else out[0]


def device_table():
    even, odd = dict(EVEN), dict(ODD)
    places = []
    for p in range(8):
        slots = [p, even[p], odd[p], odd[even[p]], even[odd[p]], even[odd[even[p]]], odd[even[odd[p]]]]
        places.append(slots + [sum(range(8)) - sum(slots)])
    every = [places[p] + [v ^ s for s in (3, 1, 2, 0)] for p in range(8) for v in range(4)]
    me = lax.axis_index(("pair", "virt"))
    return lax.dynamic_index_in_dim(jnp.array(every, jnp.int32), me, keepdims=False)


def scheduled(amplitudes, tile_mask, integrals, pair_energy, virt_energy):
    table = device_table()
    columns = integrals.shape[2]
    span_a, span_b = (0, columns // 2), (columns // 2, columns)

    def part(v, span):
        return v[:, :, span[0] : span[1]]

    e1 = over_pair(integrals, EVEN)
    o1a, o1b = over_pair(part(integrals, span_a), ODD), over_pair(part(integrals, span_b), ODD)
    a = arranged(amplitudes, tile_mask)
    o1b, a, table = tie(o1b, a, table)
    e2a, o2a = over_pair(o1a, EVEN), over_pair(part(e1, span_a), ODD)
    e2b, o2b = over_pair(o1b, EVEN), over_pair(part(e1, span_b), ODD)
    total = products(table, [0, 1, 2], a, [integrals, e1, [o1a, o1b]], (0, columns))
    o2a, e2a, total = tie(o2a, e2a, total)
    e3a, o3a = over_pair(o2a, EVEN), over_pair(e2a, ODD)
    e3b, o3b = over_pair(o2b, EVEN), over_pair(e2b, ODD)
    total = products(table, [3, 4], a, [[e2a, e2b], [o2a, o2b]], (0, columns), total=total)
    e3a, o3a, total = tie(e3a, o3a, total)
    last_a = over_pair(o3a, EVEN)
    total_a = products(table, [5, 6], a, [e3a, o3a], span_a, total=total, weight=20)
    e3b, total_a = tie(e3b, total_a)
    last_b = over_pair(e3b, ODD)
    total_b = products(table, [5, 6], a, [e3b, o3b], span_b, total=total)

    here_a, keep_there_a, keep_here_a, there_a = products(
        table, [7], a, [last_a], span_a, total=total_a, finish=True
    )
    got_there_a = over_virt(there_a, CORE)
    here_b, keep_there_b, keep_here_b, there_b = products(
        table, [7], a, [last_b], span_b, total=total_b, finish=True, weight=20
    )
    mine_a = added(keep_there_a, got_there_a)
    mine_a, there_b = tie(mine_a, there_b)
    from_y_a = over_virt(mine_a, YHOP)
    got_there_b = over_virt(there_b, CORE)
    from_y_b = over_virt(added(keep_there_b, got_there_b), YHOP)
    got_here_a, got_here_b = over_virt(here_a, CORE), over_virt(here_b, CORE)

    ladder = jnp.concatenate(
        [
            keep_here_a + got_here_a.astype(F32) + from_y_a.astype(F32),
            keep_here_b + got_here_b.astype(F32) + from_y_b.astype(F32),
        ],
        axis=1,
    )
    denom = virt_energy[None, :] - pair_energy[:, None]
    return (ladder / denom).astype(BF16)


def solution(mesh):
    placed = (
        P("pair", "virt", None),
        P("pair", "virt"),
        P("virt", "pair", None),
        P(("pair", "virt")),
        P(),
    )
    here = mesh.shape["pair"] == 8 and mesh.shape["virt"] == 4
    return jax.shard_map(
        scheduled if here else plain,
        mesh=mesh,
        in_specs=placed,
        out_specs=P(("pair", "virt"), None),
        check_vma=False,
    )
```

```python
import jax
import jax.numpy as jnp
from jax import lax
from jax.experimental import pallas as pl
from jax.experimental.pallas import tpu as pltpu
from jax.sharding import PartitionSpec as P

BF16 = jnp.bfloat16
F32 = jnp.float32


def plain(amplitudes, tile_mask, integrals, pair_energy, virt_energy):
    masked = amplitudes * tile_mask.astype(BF16)[:, :, None]
    partial_value = jnp.einsum(
        "ptk,tkn->pn",
        masked,
        lax.all_gather(integrals, "pair", axis=1, tiled=True),
        preferred_element_type=F32,
    )
    ladder = lax.psum_scatter(partial_value.astype(BF16), "virt", scatter_dimension=0, tiled=True).astype(F32)
    denom = virt_energy[None, :] - pair_energy[:, None]
    return (ladder / denom).astype(BF16)


RING = [0, 2, 4, 6, 7, 5, 3, 1]
EVEN = [(RING[i], RING[i ^ 1]) for i in range(8)]
ODD = [(RING[i], RING[(i + 2 * (i % 2) - 1) % 8]) for i in range(8)]
CORE = [(0, 1), (1, 0), (2, 3), (3, 2)]
YHOP = [(0, 2), (2, 0), (1, 3), (3, 1)]


def over_pair(value, hops):
    return lax.ppermute(value, "pair", hops)


def over_virt(value, hops):
    return lax.ppermute(value, "virt", hops)


def arranged(amplitudes, tile_mask):
    pairs, tiles, wide = amplitudes.shape
    rows = 128

    def body(amplitudes_ref, mask_ref, out_ref):
        apart = lax.broadcasted_iota(jnp.int32, (rows, rows * tiles), 1) - tiles * lax.broadcasted_iota(
            jnp.int32, (rows, rows * tiles), 0
        )
        for at in range(0, pairs, rows):
            here = pl.ds(at, rows)
            mixed = amplitudes_ref[here].reshape(rows * tiles, wide)
            mask = jnp.transpose(jnp.concatenate([mask_ref[:, here].astype(F32)] * (8 // tiles), axis=0))
            for t in range(tiles):
                chosen = jnp.where(apart == t, mask[:, t : t + 1], 0.0).astype(BF16)
                out_ref[t, here] = jnp.dot(chosen, mixed, preferred_element_type=F32).astype(BF16)

    vmem = pl.BlockSpec(memory_space=pltpu.VMEM)
    return pl.pallas_call(
        body,
        in_specs=[vmem, vmem],
        out_specs=vmem,
        out_shape=jax.ShapeDtypeStruct((tiles, pairs, wide), BF16),
        compiler_params=pltpu.CompilerParams(vmem_limit_bytes=12 * 2**20),
        cost_estimate=pl.CostEstimate(
            flops=4 * rows * tiles * amplitudes.size, bytes_accessed=4 * amplitudes.size, transcendentals=0
        ),
    )(amplitudes, tile_mask.T)


def added(kept, got):
    def body(kept_ref, *refs):
        for n, ref in enumerate(refs[:-1]):
            here = pl.ds(n * ref.shape[0], ref.shape[0])
            refs[-1][here] = (kept_ref[here] + ref[...].astype(F32)).astype(BF16)

    vmem = pl.BlockSpec(memory_space=pltpu.VMEM)
    return pl.pallas_call(
        body,
        in_specs=[vmem] * (1 + len(got)),
        out_specs=vmem,
        out_shape=jax.ShapeDtypeStruct(kept.shape, BF16),
        compiler_params=pltpu.CompilerParams(vmem_limit_bytes=4 * 2**20),
        cost_estimate=pl.CostEstimate(flops=0, bytes_accessed=0, transcendentals=0),
    )(kept, *got)


def quotient(kept, got, from_y, pair_energy, virt_energy, span, left=None, weight=1):
    rows = kept.shape[0]

    def body(kept_ref, got_ref, from_y_ref, pair_ref, virt_ref, *refs):
        out_ref = refs[-1]
        pair = jnp.transpose(jnp.concatenate([pair_ref[...]] * 8, axis=0))[:, :1]
        ladder = kept_ref[...] + got_ref[...].astype(F32) + from_y_ref[...].astype(F32)
        value = (ladder / (virt_ref[:, span[0] : span[1]] - pair)).astype(BF16)
        if left is None:
            out_ref[...] = value
        else:
            out_ref[:, : span[0]] = refs[0][...]
            out_ref[:, span[0] :] = value

    vmem = pl.BlockSpec(memory_space=pltpu.VMEM)
    more = [] if left is None else [left]
    return pl.pallas_call(
        body,
        in_specs=[vmem] * (5 + len(more)),
        out_specs=vmem,
        out_shape=jax.ShapeDtypeStruct((rows, span[1] - (span[0] if left is None else 0)), BF16),
        compiler_params=pltpu.CompilerParams(vmem_limit_bytes=8 * 2**20),
        cost_estimate=pl.CostEstimate(flops=weight * 10**8, bytes_accessed=weight * 10**6, transcendentals=0),
    )(kept, got, from_y, pair_energy[None, :], virt_energy[None, :], *more)


def tie(*values):
    return lax.optimization_barrier(values)


def products(table, slots, a, blocks, span, total=None, finish=0, weight=1):
    blocks = [b if isinstance(b, list) else [b] for b in blocks]
    flat = [v for b in blocks for v in b]
    tiles, depth = flat[0].shape[:2]
    lo, hi = span
    columns = hi - lo
    row = a.shape[1] // 4

    def body(table_ref, a_ref, *refs):
        ins, outs = list(refs[: len(flat)]), refs[len(flat):]
        if total is not None:
            total_ref, outs = outs[0], outs[1:]
        groups = [[ins.pop(0) for _ in b] for b in blocks]
        for i in range(4):
            here = pl.ds(pl.multiple_of(table_ref[8 + i] * row, row), row)
            left, right = [], []
            for slot, group in zip(slots, groups):
                cols = pl.ds(pl.multiple_of(table_ref[slot] * depth, depth), depth)
                left += [a_ref[t, here, cols] for t in range(tiles)]
                sides = [r[:, :, lo:hi] if len(group) == 1 and r.shape[2] > columns else r[...] for r in group]
                block = sides[0] if len(sides) == 1 else jnp.concatenate(sides, axis=2)
                right.append(block.reshape(tiles * depth, columns))
            acc = jnp.dot(
                jnp.concatenate(left, axis=1), jnp.concatenate(right, axis=0), preferred_element_type=F32
            )
            if total is not None:
                acc += total_ref[i, :, lo:hi] if total.shape[2] > columns else total_ref[i]
            if finish:
                if i > 0:
                    outs[i - 1][...] = acc.astype(outs[i - 1].dtype)
                else:
                    for n, ref in enumerate(outs[3:]):
                        ref[...] = acc[n * ref.shape[0] : (n + 1) * ref.shape[0]].astype(BF16)
            else:
                outs[0][i] = acc

    vmem = pl.BlockSpec(memory_space=pltpu.VMEM)
    smem = pl.BlockSpec(memory_space=pltpu.SMEM)
    operands = [a] + flat + ([] if total is None else [total])
    if finish:
        out_shape = [jax.ShapeDtypeStruct((row, columns), t) for t in (BF16, F32, F32)]
        out_shape += [jax.ShapeDtypeStruct((row // finish, columns), BF16)] * finish
    else:
        out_shape = [jax.ShapeDtypeStruct((4, row, columns), F32)]
    out = pl.pallas_call(
        body,
        in_specs=[smem] + [vmem] * len(operands),
        out_specs=[vmem] * len(out_shape),
        out_shape=out_shape,
        compiler_params=pltpu.CompilerParams(vmem_limit_bytes=20 * 2**20),
        cost_estimate=pl.CostEstimate(
            flops=weight * 2 * a.shape[1] * tiles * depth * len(blocks) * columns,
            bytes_accessed=min(weight, 1) * (2 * a.size + 2 * len(flat) * tiles * depth * columns),
            transcendentals=0,
        ),
    )(table, *operands)
    return out if finish else out[0]


def device_table():
    even, odd = dict(EVEN), dict(ODD)
    places = []
    for p in range(8):
        slots = [p, even[p], odd[p], odd[even[p]], even[odd[p]], even[odd[even[p]]], odd[even[odd[p]]]]
        places.append(slots + [sum(range(8)) - sum(slots)])
    every = [places[p] + [v ^ s for s in (3, 1, 2, 0)] for p in range(8) for v in range(4)]
    me = lax.axis_index(("pair", "virt"))
    return lax.dynamic_index_in_dim(jnp.array(every, jnp.int32), me, keepdims=False)


def scheduled(amplitudes, tile_mask, integrals, pair_energy, virt_energy):
    table = device_table()
    columns = integrals.shape[2]
    span_a, span_b = (0, columns // 2), (columns // 2, columns)

    def part(v, span):
        return v[:, :, span[0] : span[1]]

    e1 = over_pair(integrals, EVEN)
    o1a, o1b = over_pair(part(integrals, span_a), ODD), over_pair(part(integrals, span_b), ODD)
    a = arranged(amplitudes, tile_mask)
    o1b, a, table = tie(o1b, a, table)
    e2a, o2a = over_pair(o1a, EVEN), over_pair(part(e1, span_a), ODD)
    e2b, o2b = over_pair(o1b, EVEN), over_pair(part(e1, span_b), ODD)
    total = products(table, [0, 1, 2], a, [integrals, e1, [o1a, o1b]], (0, columns))
    o2a, e2a, total = tie(o2a, e2a, total)
    e3a, o3a = over_pair(o2a, EVEN), over_pair(e2a, ODD)
    e3b, o3b = over_pair(o2b, EVEN), over_pair(e2b, ODD)
    total = products(table, [3, 4], a, [[e2a, e2b], [o2a, o2b]], (0, columns), total=total)
    e3a, o3a, total = tie(e3a, o3a, total)
    last_a = over_pair(o3a, EVEN)
    total_a = products(table, [5, 6], a, [e3a, o3a], span_a, total=total, weight=20)
    e3b, total_a = tie(e3b, total_a)
    last_b = over_pair(e3b, ODD)
    total_b = products(table, [5, 6], a, [e3b, o3b], span_b, total=total)
    last_a, total_b = tie(last_a, total_b)

    here_a, keep_there_a, keep_here_a, *there_a = products(
        table, [7], a, [last_a], span_a, total=total_a, finish=2, weight=0
    )
    got_there_a = [over_virt(v, CORE) for v in there_a]
    got_there_a[0], total_b = tie(got_there_a[0], total_b)
    mine_a = added(keep_there_a, got_there_a)
    here_b, keep_there_b, keep_here_b, *there_b = products(
        table, [7], a, [last_b], span_b, total=total_b, finish=2, weight=20
    )
    from_y_a = over_virt(mine_a, YHOP)
    got_there_b = [over_virt(v, CORE) for v in there_b]
    from_y_b = over_virt(added(keep_there_b, got_there_b), YHOP)
    got_here_a, got_here_b = over_virt(here_a, CORE), over_virt(here_b, CORE)
    left = quotient(keep_here_a, got_here_a, from_y_a, pair_energy, virt_energy, span_a, weight=20)
    from_y_b, left = tie(from_y_b, left)
    return quotient(keep_here_b, got_here_b, from_y_b, pair_energy, virt_energy, span_b, left=left)


def solution(mesh):
    placed = (
        P("pair", "virt", None),
        P("pair", "virt"),
        P("virt", "pair", None),
        P(("pair", "virt")),
        P(),
    )
    here = mesh.shape["pair"] == 8 and mesh.shape["virt"] == 4
    return jax.shard_map(
        scheduled if here else plain,
        mesh=mesh,
        in_specs=placed,
        out_specs=P(("pair", "virt"), None),
        check_vma=False,
    )
```

```python
import jax
import jax.numpy as jnp
from jax import lax
from jax.experimental import pallas as pl
from jax.experimental.pallas import tpu as pltpu
from jax.sharding import PartitionSpec as P

BF16 = jnp.bfloat16
F32 = jnp.float32


def plain(amplitudes, tile_mask, integrals, pair_energy, virt_energy):
    masked = amplitudes * tile_mask.astype(BF16)[:, :, None]
    partial_value = jnp.einsum(
        "ptk,tkn->pn",
        masked,
        lax.all_gather(integrals, "pair", axis=1, tiled=True),
        preferred_element_type=F32,
    )
    ladder = lax.psum_scatter(partial_value.astype(BF16), "virt", scatter_dimension=0, tiled=True).astype(F32)
    denom = virt_energy[None, :] - pair_energy[:, None]
    return (ladder / denom).astype(BF16)


RING = [0, 2, 4, 6, 7, 5, 3, 1]
EVEN = [(RING[i], RING[i ^ 1]) for i in range(8)]
ODD = [(RING[i], RING[(i + 2 * (i % 2) - 1) % 8]) for i in range(8)]
CORE = [(0, 1), (1, 0), (2, 3), (3, 2)]
YHOP = [(0, 2), (2, 0), (1, 3), (3, 1)]


def over_pair(value, hops):
    return lax.ppermute(value, "pair", hops)


def over_virt(value, hops):
    return lax.ppermute(value, "virt", hops)


def arranged(amplitudes, tile_mask):
    pairs, tiles, wide = amplitudes.shape
    rows = 128

    def body(amplitudes_ref, mask_ref, out_ref):
        apart = lax.broadcasted_iota(jnp.int32, (rows, rows * tiles), 1) - tiles * lax.broadcasted_iota(
            jnp.int32, (rows, rows * tiles), 0
        )
        for at in range(0, pairs, rows):
            here = pl.ds(at, rows)
            mixed = amplitudes_ref[here].reshape(rows * tiles, wide)
            mask = jnp.transpose(jnp.concatenate([mask_ref[:, here].astype(F32)] * (8 // tiles), axis=0))
            for t in range(tiles):
                chosen = jnp.where(apart == t, mask[:, t : t + 1], 0.0).astype(BF16)
                out_ref[t, here] = jnp.dot(chosen, mixed, preferred_element_type=F32).astype(BF16)

    vmem = pl.BlockSpec(memory_space=pltpu.VMEM)
    return pl.pallas_call(
        body,
        in_specs=[vmem, vmem],
        out_specs=vmem,
        out_shape=jax.ShapeDtypeStruct((tiles, pairs, wide), BF16),
        compiler_params=pltpu.CompilerParams(vmem_limit_bytes=12 * 2**20),
        cost_estimate=pl.CostEstimate(
            flops=4 * rows * tiles * amplitudes.size, bytes_accessed=4 * amplitudes.size, transcendentals=0
        ),
    )(amplitudes, tile_mask.T)


def added(kept, got):
    def body(kept_ref, *refs):
        for n, ref in enumerate(refs[:-1]):
            here = pl.ds(n * ref.shape[0], ref.shape[0])
            refs[-1][here] = (kept_ref[here] + ref[...].astype(F32)).astype(BF16)

    vmem = pl.BlockSpec(memory_space=pltpu.VMEM)
    return pl.pallas_call(
        body,
        in_specs=[vmem] * (1 + len(got)),
        out_specs=vmem,
        out_shape=jax.ShapeDtypeStruct(kept.shape, BF16),
        compiler_params=pltpu.CompilerParams(vmem_limit_bytes=4 * 2**20),
        cost_estimate=pl.CostEstimate(flops=0, bytes_accessed=0, transcendentals=0),
    )(kept, *got)


def quotient(kept, got, from_y, pair_energy, virt_energy, span, left=None, weight=1):
    rows = kept.shape[0]

    def body(kept_ref, got_ref, from_y_ref, pair_ref, virt_ref, *refs):
        out_ref = refs[-1]
        pair = jnp.transpose(jnp.concatenate([pair_ref[...]] * 8, axis=0))[:, :1]
        ladder = kept_ref[...] + got_ref[...].astype(F32) + from_y_ref[...].astype(F32)
        value = (ladder / (virt_ref[:, span[0] : span[1]] - pair)).astype(BF16)
        if left is None:
            out_ref[...] = value
        else:
            out_ref[:, : span[0]] = refs[0][...]
            out_ref[:, span[0] :] = value

    vmem = pl.BlockSpec(memory_space=pltpu.VMEM)
    more = [] if left is None else [left]
    return pl.pallas_call(
        body,
        in_specs=[vmem] * (5 + len(more)),
        out_specs=vmem,
        out_shape=jax.ShapeDtypeStruct((rows, span[1] - (span[0] if left is None else 0)), BF16),
        compiler_params=pltpu.CompilerParams(vmem_limit_bytes=8 * 2**20),
        cost_estimate=pl.CostEstimate(flops=weight * 10**8, bytes_accessed=weight * 10**6, transcendentals=0),
    )(kept, got, from_y, pair_energy[None, :], virt_energy[None, :], *more)


def tie(*values):
    return lax.optimization_barrier(values)


def products(table, slots, a, blocks, span, total=None, finish=(), weight=1):
    blocks = [b if isinstance(b, list) else [b] for b in blocks]
    flat = [v for b in blocks for v in b]
    tiles, depth = flat[0].shape[:2]
    lo, hi = span
    columns = hi - lo
    row = a.shape[1] // 4
    pieces = (2, 1, 1, 1)

    def body(table_ref, a_ref, *refs):
        ins, outs = list(refs[: len(flat)]), refs[len(flat):]
        if total is not None:
            total_ref, outs = outs[0], outs[1:]
        groups = [[ins.pop(0) for _ in b] for b in blocks]
        outs = list(outs)
        for i in finish or range(4):
            here = pl.ds(pl.multiple_of(table_ref[8 + i] * row, row), row)
            left, right = [], []
            for slot, group in zip(slots, groups):
                cols = pl.ds(pl.multiple_of(table_ref[slot] * depth, depth), depth)
                left += [a_ref[t, here, cols] for t in range(tiles)]
                sides = [r[:, :, lo:hi] if len(group) == 1 and r.shape[2] > columns else r[...] for r in group]
                block = sides[0] if len(sides) == 1 else jnp.concatenate(sides, axis=2)
                right.append(block.reshape(tiles * depth, columns))
            acc = jnp.dot(
                jnp.concatenate(left, axis=1), jnp.concatenate(right, axis=0), preferred_element_type=F32
            )
            if total is not None:
                acc += total_ref[i, :, lo:hi] if total.shape[2] > columns else total_ref[i]
            if not finish:
                outs[0][i] = acc
            else:
                for n in range(pieces[i]):
                    ref = outs.pop(0)
                    ref[...] = acc[n * ref.shape[0] : (n + 1) * ref.shape[0]].astype(ref.dtype)

    vmem = pl.BlockSpec(memory_space=pltpu.VMEM)
    smem = pl.BlockSpec(memory_space=pltpu.SMEM)
    operands = [a] + flat + ([] if total is None else [total])
    if finish:
        types = (BF16, BF16, F32, F32)
        out_shape = [
            jax.ShapeDtypeStruct((row // pieces[i], columns), types[i]) for i in finish for _ in range(pieces[i])
        ]
    else:
        out_shape = [jax.ShapeDtypeStruct((4, row, columns), F32)]
    out = pl.pallas_call(
        body,
        in_specs=[smem] + [vmem] * len(operands),
        out_specs=[vmem] * len(out_shape),
        out_shape=out_shape,
        compiler_params=pltpu.CompilerParams(vmem_limit_bytes=20 * 2**20),
        cost_estimate=pl.CostEstimate(
            flops=weight * 2 * row * len(finish or range(4)) * tiles * depth * len(blocks) * columns,
            bytes_accessed=min(weight, 1) * (2 * a.size + 2 * len(flat) * tiles * depth * columns),
            transcendentals=0,
        ),
    )(table, *operands)
    return out if finish else out[0]


def device_table():
    even, odd = dict(EVEN), dict(ODD)
    places = []
    for p in range(8):
        slots = [p, even[p], odd[p], odd[even[p]], even[odd[p]], even[odd[even[p]]], odd[even[odd[p]]]]
        places.append(slots + [sum(range(8)) - sum(slots)])
    every = [places[p] + [v ^ s for s in (3, 1, 2, 0)] for p in range(8) for v in range(4)]
    me = lax.axis_index(("pair", "virt"))
    return lax.dynamic_index_in_dim(jnp.array(every, jnp.int32), me, keepdims=False)


def scheduled(amplitudes, tile_mask, integrals, pair_energy, virt_energy):
    table = device_table()
    columns = integrals.shape[2]
    span_a, span_b = (0, columns // 2), (columns // 2, columns)

    def part(v, span):
        return v[:, :, span[0] : span[1]]

    e1 = over_pair(integrals, EVEN)
    o1a, o1b = over_pair(part(integrals, span_a), ODD), over_pair(part(integrals, span_b), ODD)
    a = arranged(amplitudes, tile_mask)
    o1a, a, table = tie(o1a, a, table)
    e2a, o2a = over_pair(o1a, EVEN), over_pair(part(e1, span_a), ODD)
    e2b, o2b = over_pair(o1b, EVEN), over_pair(part(e1, span_b), ODD)
    total = products(table, [0, 1, 2], a, [integrals, e1, [o1a, o1b]], (0, columns))
    o2a, e2a, total = tie(o2a, e2a, total)
    e3a, o3a = over_pair(o2a, EVEN), over_pair(e2a, ODD)
    e3b, o3b = over_pair(o2b, EVEN), over_pair(e2b, ODD)
    total = products(table, [3, 4], a, [[e2a, e2b], [o2a, o2b]], (0, columns), total=total)
    e3a, o3a, total = tie(e3a, o3a, total)
    last_a = over_pair(o3a, EVEN)
    total_a = products(table, [5, 6], a, [e3a, o3a], span_a, total=total, weight=20)
    e3b, total_a = tie(e3b, total_a)
    last_b = over_pair(e3b, ODD)

    there_a = products(table, [7], a, [last_a], span_a, total=total_a, finish=(0,), weight=0)
    got_there_a = [over_virt(v, CORE) for v in there_a]
    here_a, keep_there_a, keep_here_a = products(
        table, [7], a, [last_a], span_a, total=total_a, finish=(1, 2, 3), weight=0
    )
    mine_a = added(keep_there_a, got_there_a)
    total, mine_a = tie(total, mine_a)
    total_b = products(table, [5, 6], a, [e3b, o3b], span_b, total=total)
    there_b = products(table, [7], a, [last_b], span_b, total=total_b, finish=(0,), weight=20)
    from_y_a = over_virt(mine_a, YHOP)
    got_there_b = [over_virt(v, CORE) for v in there_b]
    here_b, keep_there_b, keep_here_b = products(
        table, [7], a, [last_b], span_b, total=total_b, finish=(1, 2, 3), weight=0
    )
    from_y_b = over_virt(added(keep_there_b, got_there_b), YHOP)
    got_here_a, got_here_b = over_virt(here_a, CORE), over_virt(here_b, CORE)
    left = quotient(keep_here_a, got_here_a, from_y_a, pair_energy, virt_energy, span_a, weight=20)
    from_y_b, left = tie(from_y_b, left)
    return quotient(keep_here_b, got_here_b, from_y_b, pair_energy, virt_energy, span_b, left=left)


def solution(mesh):
    placed = (
        P("pair", "virt", None),
        P("pair", "virt"),
        P("virt", "pair", None),
        P(("pair", "virt")),
        P(),
    )
    here = mesh.shape["pair"] == 8 and mesh.shape["virt"] == 4
    return jax.shard_map(
        scheduled if here else plain,
        mesh=mesh,
        in_specs=placed,
        out_specs=P(("pair", "virt"), None),
        check_vma=False,
    )
```

```python
import jax
import jax.numpy as jnp
from jax import lax
from jax.experimental import pallas as pl
from jax.experimental.pallas import tpu as pltpu
from jax.sharding import PartitionSpec as P

BF16 = jnp.bfloat16
F32 = jnp.float32


def plain(amplitudes, tile_mask, integrals, pair_energy, virt_energy):
    masked = amplitudes * tile_mask.astype(BF16)[:, :, None]
    partial_value = jnp.einsum(
        "ptk,tkn->pn",
        masked,
        lax.all_gather(integrals, "pair", axis=1, tiled=True),
        preferred_element_type=F32,
    )
    ladder = lax.psum_scatter(partial_value.astype(BF16), "virt", scatter_dimension=0, tiled=True).astype(F32)
    denom = virt_energy[None, :] - pair_energy[:, None]
    return (ladder / denom).astype(BF16)


RING = [0, 2, 4, 6, 7, 5, 3, 1]
EVEN = [(RING[i], RING[i ^ 1]) for i in range(8)]
ODD = [(RING[i], RING[(i + 2 * (i % 2) - 1) % 8]) for i in range(8)]
CORE = [(0, 1), (1, 0), (2, 3), (3, 2)]
YHOP = [(0, 2), (2, 0), (1, 3), (3, 1)]


def over_pair(value, hops):
    return lax.ppermute(value, "pair", hops)


def over_virt(value, hops):
    return lax.ppermute(value, "virt", hops)


def arranged(amplitudes, tile_mask):
    pairs, tiles, wide = amplitudes.shape
    rows = 128

    def body(amplitudes_ref, mask_ref, out_ref):
        apart = lax.broadcasted_iota(jnp.int32, (rows, rows * tiles), 1) - tiles * lax.broadcasted_iota(
            jnp.int32, (rows, rows * tiles), 0
        )
        for at in range(0, pairs, rows):
            here = pl.ds(at, rows)
            mixed = amplitudes_ref[here].reshape(rows * tiles, wide)
            mask = jnp.transpose(jnp.concatenate([mask_ref[:, here].astype(F32)] * (8 // tiles), axis=0))
            for t in range(tiles):
                chosen = jnp.where(apart == t, mask[:, t : t + 1], 0.0).astype(BF16)
                out_ref[t, here] = jnp.dot(chosen, mixed, preferred_element_type=F32).astype(BF16)

    vmem = pl.BlockSpec(memory_space=pltpu.VMEM)
    return pl.pallas_call(
        body,
        in_specs=[vmem, vmem],
        out_specs=vmem,
        out_shape=jax.ShapeDtypeStruct((tiles, pairs, wide), BF16),
        compiler_params=pltpu.CompilerParams(vmem_limit_bytes=12 * 2**20),
        cost_estimate=pl.CostEstimate(
            flops=4 * rows * tiles * amplitudes.size, bytes_accessed=4 * amplitudes.size, transcendentals=0
        ),
    )(amplitudes, tile_mask.T)


def added(kept, got):
    def body(kept_ref, *refs):
        for n, ref in enumerate(refs[:-1]):
            here = pl.ds(n * ref.shape[0], ref.shape[0])
            refs[-1][here] = (kept_ref[here] + ref[...].astype(F32)).astype(BF16)

    vmem = pl.BlockSpec(memory_space=pltpu.VMEM)
    return pl.pallas_call(
        body,
        in_specs=[vmem] * (1 + len(got)),
        out_specs=vmem,
        out_shape=jax.ShapeDtypeStruct(kept.shape, BF16),
        compiler_params=pltpu.CompilerParams(vmem_limit_bytes=4 * 2**20),
        cost_estimate=pl.CostEstimate(flops=0, bytes_accessed=0, transcendentals=0),
    )(kept, *got)


def first_quotient(kept, got, from_y, pair_energy, virt_energy, span):
    rows, columns = kept.shape
    rest = virt_energy.shape[0] - span[1]

    def body(kept_ref, got_ref, from_y_ref, pair_ref, virt_ref, out_ref, inverse_ref):
        pair = jnp.transpose(jnp.concatenate([pair_ref[...]] * 8, axis=0))[:, :1]
        ladder = kept_ref[...] + got_ref[...].astype(F32) + from_y_ref[...].astype(F32)
        out_ref[...] = (ladder / (virt_ref[:, : span[1]] - pair)).astype(BF16)
        inverse_ref[...] = 1.0 / (virt_ref[:, span[1] :] - pair)

    vmem = pl.BlockSpec(memory_space=pltpu.VMEM)
    return pl.pallas_call(
        body,
        in_specs=[vmem] * 5,
        out_specs=[vmem, vmem],
        out_shape=[jax.ShapeDtypeStruct((rows, columns), BF16), jax.ShapeDtypeStruct((rows, rest), F32)],
        compiler_params=pltpu.CompilerParams(vmem_limit_bytes=8 * 2**20),
        cost_estimate=pl.CostEstimate(flops=2 * 10**9, bytes_accessed=2 * 10**7, transcendentals=0),
    )(kept, got, from_y, pair_energy[None, :], virt_energy[None, :])


def second_quotient(kept, got, from_y, inverse, left):
    rows, columns = kept.shape
    at = left.shape[1]

    def body(kept_ref, got_ref, from_y_ref, inverse_ref, left_ref, out_ref):
        out_ref[:, :at] = left_ref[...]
        ladder = kept_ref[...] + got_ref[...].astype(F32) + from_y_ref[...].astype(F32)
        out_ref[:, at:] = (ladder * inverse_ref[...]).astype(BF16)

    vmem = pl.BlockSpec(memory_space=pltpu.VMEM)
    return pl.pallas_call(
        body,
        in_specs=[vmem] * 5,
        out_specs=vmem,
        out_shape=jax.ShapeDtypeStruct((rows, at + columns), BF16),
        compiler_params=pltpu.CompilerParams(vmem_limit_bytes=8 * 2**20),
        cost_estimate=pl.CostEstimate(flops=10**8, bytes_accessed=10**6, transcendentals=0),
    )(kept, got, from_y, inverse, left)


def tie(*values):
    return lax.optimization_barrier(values)


def products(table, slots, a, blocks, span, total=None, finish=(), weight=1):
    blocks = [b if isinstance(b, list) else [b] for b in blocks]
    flat = [v for b in blocks for v in b]
    tiles, depth = flat[0].shape[:2]
    lo, hi = span
    columns = hi - lo
    row = a.shape[1] // 4
    pieces = (2, 1, 1, 1)

    def body(table_ref, a_ref, *refs):
        ins, outs = list(refs[: len(flat)]), refs[len(flat):]
        if total is not None:
            total_ref, outs = outs[0], outs[1:]
        groups = [[ins.pop(0) for _ in b] for b in blocks]
        outs = list(outs)
        for i in finish or range(4):
            here = pl.ds(pl.multiple_of(table_ref[8 + i] * row, row), row)
            left, right = [], []
            for slot, group in zip(slots, groups):
                cols = pl.ds(pl.multiple_of(table_ref[slot] * depth, depth), depth)
                left += [a_ref[t, here, cols] for t in range(tiles)]
                sides = [r[:, :, lo:hi] if len(group) == 1 and r.shape[2] > columns else r[...] for r in group]
                block = sides[0] if len(sides) == 1 else jnp.concatenate(sides, axis=2)
                right.append(block.reshape(tiles * depth, columns))
            acc = jnp.dot(
                jnp.concatenate(left, axis=1), jnp.concatenate(right, axis=0), preferred_element_type=F32
            )
            if total is not None:
                acc += total_ref[i, :, lo:hi] if total.shape[2] > columns else total_ref[i]
            if not finish:
                outs[0][i] = acc
            else:
                for n in range(pieces[i]):
                    ref = outs.pop(0)
                    ref[...] = acc[n * ref.shape[0] : (n + 1) * ref.shape[0]].astype(ref.dtype)

    vmem = pl.BlockSpec(memory_space=pltpu.VMEM)
    smem = pl.BlockSpec(memory_space=pltpu.SMEM)
    operands = [a] + flat + ([] if total is None else [total])
    if finish:
        types = (BF16, BF16, F32, F32)
        out_shape = [
            jax.ShapeDtypeStruct((row // pieces[i], columns), types[i]) for i in finish for _ in range(pieces[i])
        ]
    else:
        out_shape = [jax.ShapeDtypeStruct((4, row, columns), F32)]
    out = pl.pallas_call(
        body,
        in_specs=[smem] + [vmem] * len(operands),
        out_specs=[vmem] * len(out_shape),
        out_shape=out_shape,
        compiler_params=pltpu.CompilerParams(vmem_limit_bytes=20 * 2**20),
        cost_estimate=pl.CostEstimate(
            flops=weight * 2 * row * len(finish or range(4)) * tiles * depth * len(blocks) * columns,
            bytes_accessed=min(weight, 1) * (2 * a.size + 2 * len(flat) * tiles * depth * columns),
            transcendentals=0,
        ),
    )(table, *operands)
    return out if finish else out[0]


def device_table():
    even, odd = dict(EVEN), dict(ODD)
    places = []
    for p in range(8):
        slots = [p, even[p], odd[p], odd[even[p]], even[odd[p]], even[odd[even[p]]], odd[even[odd[p]]]]
        places.append(slots + [sum(range(8)) - sum(slots)])
    every = [places[p] + [v ^ s for s in (3, 1, 2, 0)] for p in range(8) for v in range(4)]
    me = lax.axis_index(("pair", "virt"))
    return lax.dynamic_index_in_dim(jnp.array(every, jnp.int32), me, keepdims=False)


def scheduled(amplitudes, tile_mask, integrals, pair_energy, virt_energy):
    table = device_table()
    columns = integrals.shape[2]
    span_a, span_b = (0, columns // 2), (columns // 2, columns)

    def part(v, span):
        return v[:, :, span[0] : span[1]]

    e1 = over_pair(integrals, EVEN)
    o1a, o1b = over_pair(part(integrals, span_a), ODD), over_pair(part(integrals, span_b), ODD)
    a = arranged(amplitudes, tile_mask)
    o1a, a, table = tie(o1a, a, table)
    e2a, o2a = over_pair(o1a, EVEN), over_pair(part(e1, span_a), ODD)
    e2b, o2b = over_pair(o1b, EVEN), over_pair(part(e1, span_b), ODD)
    total = products(table, [0, 1, 2], a, [integrals, e1, [o1a, o1b]], (0, columns))
    o2a, e2a, total = tie(o2a, e2a, total)
    e3a, o3a = over_pair(o2a, EVEN), over_pair(e2a, ODD)
    e3b, o3b = over_pair(o2b, EVEN), over_pair(e2b, ODD)
    total = products(table, [3, 4], a, [[e2a, e2b], [o2a, o2b]], (0, columns), total=total)
    e3a, o3a, total = tie(e3a, o3a, total)
    last_a = over_pair(o3a, EVEN)
    total_a = products(table, [5, 6], a, [e3a, o3a], span_a, total=total, weight=20)
    e3b, total_a = tie(e3b, total_a)
    last_b = over_pair(e3b, ODD)

    there_a = products(table, [7], a, [last_a], span_a, total=total_a, finish=(0,), weight=0)
    got_there_a = [over_virt(v, CORE) for v in there_a]
    here_a, keep_there_a, keep_here_a = products(
        table, [7], a, [last_a], span_a, total=total_a, finish=(1, 2, 3), weight=0
    )
    mine_a = added(keep_there_a, got_there_a)
    total, mine_a = tie(total, mine_a)
    total_b = products(table, [5, 6], a, [e3b, o3b], span_b, total=total)
    there_b = products(table, [7], a, [last_b], span_b, total=total_b, finish=(0,), weight=20)
    from_y_a = over_virt(mine_a, YHOP)
    got_there_b = [over_virt(v, CORE) for v in there_b]
    here_b, keep_there_b, keep_here_b = products(
        table, [7], a, [last_b], span_b, total=total_b, finish=(1, 2, 3), weight=0
    )
    from_y_b = over_virt(added(keep_there_b, got_there_b), YHOP)
    got_here_a, got_here_b = over_virt(here_a, CORE), over_virt(here_b, CORE)
    left, inverse = first_quotient(keep_here_a, got_here_a, from_y_a, pair_energy, virt_energy, span_a)
    from_y_b, left = tie(from_y_b, left)
    return second_quotient(keep_here_b, got_here_b, from_y_b, inverse, left)


def solution(mesh):
    placed = (
        P("pair", "virt", None),
        P("pair", "virt"),
        P("virt", "pair", None),
        P(("pair", "virt")),
        P(),
    )
    here = mesh.shape["pair"] == 8 and mesh.shape["virt"] == 4
    return jax.shard_map(
        scheduled if here else plain,
        mesh=mesh,
        in_specs=placed,
        out_specs=P(("pair", "virt"), None),
        check_vma=False,
    )
```

```python
import jax
import jax.numpy as jnp
from jax import lax
from jax.experimental import pallas as pl
from jax.experimental.pallas import tpu as pltpu
from jax.sharding import PartitionSpec as P

BF16 = jnp.bfloat16
F32 = jnp.float32


def plain(amplitudes, tile_mask, integrals, pair_energy, virt_energy):
    masked = amplitudes * tile_mask.astype(BF16)[:, :, None]
    partial_value = jnp.einsum(
        "ptk,tkn->pn",
        masked,
        lax.all_gather(integrals, "pair", axis=1, tiled=True),
        preferred_element_type=F32,
    )
    ladder = lax.psum_scatter(partial_value.astype(BF16), "virt", scatter_dimension=0, tiled=True).astype(F32)
    denom = virt_energy[None, :] - pair_energy[:, None]
    return (ladder / denom).astype(BF16)


RING = [0, 2, 4, 6, 7, 5, 3, 1]
EVEN = [(RING[i], RING[i ^ 1]) for i in range(8)]
ODD = [(RING[i], RING[(i + 2 * (i % 2) - 1) % 8]) for i in range(8)]
CORE = [(0, 1), (1, 0), (2, 3), (3, 2)]
YHOP = [(0, 2), (2, 0), (1, 3), (3, 1)]


def over_pair(value, hops):
    return lax.ppermute(value, "pair", hops)


def over_virt(value, hops):
    return lax.ppermute(value, "virt", hops)


def arranged(amplitudes, tile_mask):
    pairs, tiles, wide = amplitudes.shape
    rows = 128

    def body(amplitudes_ref, mask_ref, out_ref):
        apart = lax.broadcasted_iota(jnp.int32, (rows, rows * tiles), 1) - tiles * lax.broadcasted_iota(
            jnp.int32, (rows, rows * tiles), 0
        )
        for at in range(0, pairs, rows):
            here = pl.ds(at, rows)
            mixed = amplitudes_ref[here].reshape(rows * tiles, wide)
            mask = jnp.transpose(jnp.concatenate([mask_ref[:, here].astype(F32)] * (8 // tiles), axis=0))
            for t in range(tiles):
                chosen = jnp.where(apart == t, mask[:, t : t + 1], 0.0).astype(BF16)
                out_ref[t, here] = jnp.dot(chosen, mixed, preferred_element_type=F32).astype(BF16)

    vmem = pl.BlockSpec(memory_space=pltpu.VMEM)
    return pl.pallas_call(
        body,
        in_specs=[vmem, vmem],
        out_specs=vmem,
        out_shape=jax.ShapeDtypeStruct((tiles, pairs, wide), BF16),
        compiler_params=pltpu.CompilerParams(vmem_limit_bytes=12 * 2**20),
        cost_estimate=pl.CostEstimate(
            flops=4 * rows * tiles * amplitudes.size, bytes_accessed=4 * amplitudes.size, transcendentals=0
        ),
    )(amplitudes, tile_mask.T)


def added(kept, got):
    def body(kept_ref, *refs):
        for n, ref in enumerate(refs[:-1]):
            here = pl.ds(n * ref.shape[0], ref.shape[0])
            refs[-1][here] = (kept_ref[here] + ref[...].astype(F32)).astype(BF16)

    vmem = pl.BlockSpec(memory_space=pltpu.VMEM)
    return pl.pallas_call(
        body,
        in_specs=[vmem] * (1 + len(got)),
        out_specs=vmem,
        out_shape=jax.ShapeDtypeStruct(kept.shape, BF16),
        compiler_params=pltpu.CompilerParams(vmem_limit_bytes=4 * 2**20),
        cost_estimate=pl.CostEstimate(flops=0, bytes_accessed=0, transcendentals=0),
    )(kept, *got)


def first_quotient(kept, got, from_y, pair_energy, virt_energy, span):
    rows, columns = kept.shape
    rest = virt_energy.shape[0] - span[1]

    def body(kept_ref, got_ref, from_y_ref, pair_ref, virt_ref, out_ref, inverse_ref):
        pair = jnp.transpose(jnp.concatenate([pair_ref[...]] * 8, axis=0))[:, :1]
        ladder = kept_ref[...] + got_ref[...].astype(F32) + from_y_ref[...].astype(F32)
        out_ref[...] = (ladder / (virt_ref[:, : span[1]] - pair)).astype(BF16)
        inverse_ref[...] = 1.0 / (virt_ref[:, span[1] :] - pair)

    vmem = pl.BlockSpec(memory_space=pltpu.VMEM)
    return pl.pallas_call(
        body,
        in_specs=[vmem] * 5,
        out_specs=[vmem, vmem],
        out_shape=[jax.ShapeDtypeStruct((rows, columns), BF16), jax.ShapeDtypeStruct((rows, rest), F32)],
        compiler_params=pltpu.CompilerParams(vmem_limit_bytes=8 * 2**20),
        cost_estimate=pl.CostEstimate(flops=2 * 10**9, bytes_accessed=2 * 10**7, transcendentals=0),
    )(kept, got, from_y, pair_energy[None, :], virt_energy[None, :])


def second_quotient(kept, got, from_y, inverse, left):
    rows, columns = kept.shape
    at = left.shape[1]

    def body(kept_ref, got_ref, from_y_ref, inverse_ref, left_ref, out_ref):
        out_ref[:, :at] = left_ref[...]
        ladder = kept_ref[...] + got_ref[...].astype(F32) + from_y_ref[...].astype(F32)
        out_ref[:, at:] = (ladder * inverse_ref[...]).astype(BF16)

    vmem = pl.BlockSpec(memory_space=pltpu.VMEM)
    return pl.pallas_call(
        body,
        in_specs=[vmem] * 5,
        out_specs=vmem,
        out_shape=jax.ShapeDtypeStruct((rows, at + columns), BF16),
        compiler_params=pltpu.CompilerParams(vmem_limit_bytes=8 * 2**20),
        cost_estimate=pl.CostEstimate(flops=10**8, bytes_accessed=10**6, transcendentals=0),
    )(kept, got, from_y, inverse, left)


def tie(*values):
    return lax.optimization_barrier(values)


def products(table, slots, a, blocks, span, total=None, finish=(), weight=1):
    blocks = [b if isinstance(b, list) else [b] for b in blocks]
    flat = [v for b in blocks for v in b]
    tiles, depth = flat[0].shape[:2]
    lo, hi = span
    columns = hi - lo
    row = a.shape[1] // 4
    pieces = (2, 1, 1, 1)

    def body(table_ref, a_ref, *refs):
        ins, outs = list(refs[: len(flat)]), refs[len(flat):]
        if total is not None:
            total_ref, outs = outs[0], outs[1:]
        groups = [[ins.pop(0) for _ in b] for b in blocks]
        outs = list(outs)
        for i in finish or range(4):
            here = pl.ds(pl.multiple_of(table_ref[8 + i] * row, row), row)
            left, right = [], []
            for slot, group in zip(slots, groups):
                cols = pl.ds(pl.multiple_of(table_ref[slot] * depth, depth), depth)
                left += [a_ref[t, here, cols] for t in range(tiles)]
                sides = [r[:, :, lo:hi] if len(group) == 1 and r.shape[2] > columns else r[...] for r in group]
                block = sides[0] if len(sides) == 1 else jnp.concatenate(sides, axis=2)
                right.append(block.reshape(tiles * depth, columns))
            acc = jnp.dot(
                jnp.concatenate(left, axis=1), jnp.concatenate(right, axis=0), preferred_element_type=F32
            )
            if total is not None:
                acc += total_ref[i, :, lo:hi] if total.shape[2] > columns else total_ref[i]
            if not finish:
                outs[0][i] = acc
            else:
                for n in range(pieces[i]):
                    ref = outs.pop(0)
                    ref[...] = acc[n * ref.shape[0] : (n + 1) * ref.shape[0]].astype(ref.dtype)

    vmem = pl.BlockSpec(memory_space=pltpu.VMEM)
    smem = pl.BlockSpec(memory_space=pltpu.SMEM)
    operands = [a] + flat + ([] if total is None else [total])
    if finish:
        types = (BF16, BF16, F32, F32)
        out_shape = [
            jax.ShapeDtypeStruct((row // pieces[i], columns), types[i]) for i in finish for _ in range(pieces[i])
        ]
    else:
        out_shape = [jax.ShapeDtypeStruct((4, row, columns), F32)]
    out = pl.pallas_call(
        body,
        in_specs=[smem] + [vmem] * len(operands),
        out_specs=[vmem] * len(out_shape),
        out_shape=out_shape,
        compiler_params=pltpu.CompilerParams(vmem_limit_bytes=20 * 2**20),
        cost_estimate=pl.CostEstimate(
            flops=weight * 2 * row * len(finish or range(4)) * tiles * depth * len(blocks) * columns,
            bytes_accessed=min(weight, 1) * (2 * a.size + 2 * len(flat) * tiles * depth * columns),
            transcendentals=0,
        ),
    )(table, *operands)
    return out if finish else out[0]


def device_table():
    even, odd = dict(EVEN), dict(ODD)
    places = []
    for p in range(8):
        slots = [p, even[p], odd[p], odd[even[p]], even[odd[p]], even[odd[even[p]]], odd[even[odd[p]]]]
        places.append(slots + [sum(range(8)) - sum(slots)])
    every = [places[p] + [v ^ s for s in (3, 1, 2, 0)] for p in range(8) for v in range(4)]
    me = lax.axis_index(("pair", "virt"))
    return lax.dynamic_index_in_dim(jnp.array(every, jnp.int32), me, keepdims=False)


def scheduled(amplitudes, tile_mask, integrals, pair_energy, virt_energy):
    table = device_table()
    columns = integrals.shape[2]
    span_a, span_b = (0, columns // 2), (columns // 2, columns)

    def part(v, span):
        return v[:, :, span[0] : span[1]]

    e1 = over_pair(integrals, EVEN)
    o1a, o1b = over_pair(part(integrals, span_a), ODD), over_pair(part(integrals, span_b), ODD)
    a = arranged(amplitudes, tile_mask)
    o1a, a, table = tie(o1a, a, table)
    e2a, o2a = over_pair(o1a, EVEN), over_pair(part(e1, span_a), ODD)
    e2b, o2b = over_pair(o1b, EVEN), over_pair(part(e1, span_b), ODD)
    e3a, o3a = over_pair(o2a, EVEN), over_pair(e2a, ODD)
    e3b, o3b = over_pair(o2b, EVEN), over_pair(e2b, ODD)
    total = products(
        table, [0, 1, 2, 3, 4], a, [integrals, e1, [o1a, o1b], [e2a, e2b], [o2a, o2b]], (0, columns)
    )
    e3a, o3a, total = tie(e3a, o3a, total)
    last_a = over_pair(o3a, EVEN)
    total_a = products(table, [5, 6], a, [e3a, o3a], span_a, total=total, weight=20)
    e3b, total_a = tie(e3b, total_a)
    last_b = over_pair(e3b, ODD)

    there_a = products(table, [7], a, [last_a], span_a, total=total_a, finish=(0,), weight=0)
    got_there_a = [over_virt(v, CORE) for v in there_a]
    here_a, keep_there_a, keep_here_a = products(
        table, [7], a, [last_a], span_a, total=total_a, finish=(1, 2, 3), weight=0
    )
    mine_a = added(keep_there_a, got_there_a)
    total, mine_a = tie(total, mine_a)
    total_b = products(table, [5, 6], a, [e3b, o3b], span_b, total=total)
    there_b = products(table, [7], a, [last_b], span_b, total=total_b, finish=(0,), weight=20)
    from_y_a = over_virt(mine_a, YHOP)
    got_there_b = [over_virt(v, CORE) for v in there_b]
    here_b, keep_there_b, keep_here_b = products(
        table, [7], a, [last_b], span_b, total=total_b, finish=(1, 2, 3), weight=0
    )
    from_y_b = over_virt(added(keep_there_b, got_there_b), YHOP)
    got_here_a, got_here_b = over_virt(here_a, CORE), over_virt(here_b, CORE)
    left, inverse = first_quotient(keep_here_a, got_here_a, from_y_a, pair_energy, virt_energy, span_a)
    from_y_b, left = tie(from_y_b, left)
    return second_quotient(keep_here_b, got_here_b, from_y_b, inverse, left)


def solution(mesh):
    placed = (
        P("pair", "virt", None),
        P("pair", "virt"),
        P("virt", "pair", None),
        P(("pair", "virt")),
        P(),
    )
    here = mesh.shape["pair"] == 8 and mesh.shape["virt"] == 4
    return jax.shard_map(
        scheduled if here else plain,
        mesh=mesh,
        in_specs=placed,
        out_specs=P(("pair", "virt"), None),
        check_vma=False,
    )
```

```python
import jax
import jax.numpy as jnp
from jax import lax
from jax.experimental import pallas as pl
from jax.experimental.pallas import tpu as pltpu
from jax.sharding import PartitionSpec as P

BF16 = jnp.bfloat16
F32 = jnp.float32


def plain(amplitudes, tile_mask, integrals, pair_energy, virt_energy):
    masked = amplitudes * tile_mask.astype(BF16)[:, :, None]
    partial_value = jnp.einsum(
        "ptk,tkn->pn",
        masked,
        lax.all_gather(integrals, "pair", axis=1, tiled=True),
        preferred_element_type=F32,
    )
    ladder = lax.psum_scatter(partial_value.astype(BF16), "virt", scatter_dimension=0, tiled=True).astype(F32)
    denom = virt_energy[None, :] - pair_energy[:, None]
    return (ladder / denom).astype(BF16)


RING = [0, 2, 4, 6, 7, 5, 3, 1]
EVEN = [(RING[i], RING[i ^ 1]) for i in range(8)]
ODD = [(RING[i], RING[(i + 2 * (i % 2) - 1) % 8]) for i in range(8)]
CORE = [(0, 1), (1, 0), (2, 3), (3, 2)]
YHOP = [(0, 2), (2, 0), (1, 3), (3, 1)]


def over_pair(value, hops):
    return lax.ppermute(value, "pair", hops)


def over_virt(value, hops):
    return lax.ppermute(value, "virt", hops)


def arranged(amplitudes, tile_mask):
    pairs, tiles, wide = amplitudes.shape
    rows = 128

    def body(amplitudes_ref, mask_ref, out_ref):
        apart = lax.broadcasted_iota(jnp.int32, (rows, rows * tiles), 1) - tiles * lax.broadcasted_iota(
            jnp.int32, (rows, rows * tiles), 0
        )
        for at in range(0, pairs, rows):
            here = pl.ds(at, rows)
            mixed = amplitudes_ref[here].reshape(rows * tiles, wide)
            mask = jnp.transpose(jnp.concatenate([mask_ref[:, here].astype(F32)] * (8 // tiles), axis=0))
            for t in range(tiles):
                chosen = jnp.where(apart == t, mask[:, t : t + 1], 0.0).astype(BF16)
                out_ref[t, here] = jnp.dot(chosen, mixed, preferred_element_type=F32).astype(BF16)

    vmem = pl.BlockSpec(memory_space=pltpu.VMEM)
    return pl.pallas_call(
        body,
        in_specs=[vmem, vmem],
        out_specs=vmem,
        out_shape=jax.ShapeDtypeStruct((tiles, pairs, wide), BF16),
        compiler_params=pltpu.CompilerParams(vmem_limit_bytes=12 * 2**20),
        cost_estimate=pl.CostEstimate(
            flops=4 * rows * tiles * amplitudes.size, bytes_accessed=4 * amplitudes.size, transcendentals=0
        ),
    )(amplitudes, tile_mask.T)


def added(kept, got):
    def body(kept_ref, *refs):
        for n, ref in enumerate(refs[:-1]):
            here = pl.ds(n * ref.shape[0], ref.shape[0])
            refs[-1][here] = (kept_ref[here] + ref[...].astype(F32)).astype(BF16)

    vmem = pl.BlockSpec(memory_space=pltpu.VMEM)
    return pl.pallas_call(
        body,
        in_specs=[vmem] * (1 + len(got)),
        out_specs=vmem,
        out_shape=jax.ShapeDtypeStruct(kept.shape, BF16),
        compiler_params=pltpu.CompilerParams(vmem_limit_bytes=4 * 2**20),
        cost_estimate=pl.CostEstimate(flops=0, bytes_accessed=0, transcendentals=0),
    )(kept, *got)


def first_quotient(kept, got, from_y, pair_energy, virt_energy, span):
    rows, columns = kept.shape
    rest = virt_energy.shape[0] - span[1]

    def body(kept_ref, got_ref, from_y_ref, pair_ref, virt_ref, out_ref, inverse_ref):
        pair = jnp.transpose(jnp.concatenate([pair_ref[...]] * 8, axis=0))[:, :1]
        ladder = kept_ref[...] + got_ref[...].astype(F32) + from_y_ref[...].astype(F32)
        out_ref[...] = (ladder / (virt_ref[:, : span[1]] - pair)).astype(BF16)
        inverse_ref[...] = 1.0 / (virt_ref[:, span[1] :] - pair)

    vmem = pl.BlockSpec(memory_space=pltpu.VMEM)
    return pl.pallas_call(
        body,
        in_specs=[vmem] * 5,
        out_specs=[vmem, vmem],
        out_shape=[jax.ShapeDtypeStruct((rows, columns), BF16), jax.ShapeDtypeStruct((rows, rest), F32)],
        compiler_params=pltpu.CompilerParams(vmem_limit_bytes=8 * 2**20),
        cost_estimate=pl.CostEstimate(flops=2 * 10**9, bytes_accessed=2 * 10**7, transcendentals=0),
    )(kept, got, from_y, pair_energy[None, :], virt_energy[None, :])


def second_quotient(kept, got, from_y, inverse, left):
    rows, columns = kept.shape
    at = left.shape[1]

    def body(kept_ref, got_ref, from_y_ref, inverse_ref, left_ref, out_ref):
        out_ref[:, :at] = left_ref[...]
        ladder = kept_ref[...] + got_ref[...].astype(F32) + from_y_ref[...].astype(F32)
        out_ref[:, at:] = (ladder * inverse_ref[...]).astype(BF16)

    vmem = pl.BlockSpec(memory_space=pltpu.VMEM)
    return pl.pallas_call(
        body,
        in_specs=[vmem] * 5,
        out_specs=vmem,
        out_shape=jax.ShapeDtypeStruct((rows, at + columns), BF16),
        compiler_params=pltpu.CompilerParams(vmem_limit_bytes=8 * 2**20),
        cost_estimate=pl.CostEstimate(flops=10**8, bytes_accessed=10**6, transcendentals=0),
    )(kept, got, from_y, inverse, left)


def halves(integrals):
    tiles, depth, columns = integrals.shape
    half = columns // 2

    def body(in_ref, a_ref, b_ref, sem):
        copies = [
            pltpu.make_async_copy(in_ref.at[:, :, :half], a_ref, sem.at[0]),
            pltpu.make_async_copy(in_ref.at[:, :, half:], b_ref, sem.at[1]),
        ]
        for copy in copies:
            copy.start()
        for copy in copies:
            copy.wait()

    return pl.pallas_call(
        body,
        in_specs=[pl.BlockSpec(memory_space=pl.ANY)],
        out_specs=[pl.BlockSpec(memory_space=pltpu.VMEM)] * 2,
        out_shape=[jax.ShapeDtypeStruct((tiles, depth, half), BF16)] * 2,
        scratch_shapes=[pltpu.SemaphoreType.DMA((2,))],
        compiler_params=pltpu.CompilerParams(vmem_limit_bytes=4 * 2**20),
    )(integrals)


def tie(*values):
    return lax.optimization_barrier(values)


def products(table, slots, a, blocks, span, total=None, finish=(), weight=1):
    blocks = [b if isinstance(b, list) else [b] for b in blocks]
    flat = [v for b in blocks for v in b]
    tiles, depth = flat[0].shape[:2]
    lo, hi = span
    columns = hi - lo
    row = a.shape[1] // 4
    pieces = (2, 1, 1, 1)

    def body(table_ref, a_ref, *refs):
        ins, outs = list(refs[: len(flat)]), refs[len(flat):]
        if total is not None:
            total_ref, outs = outs[0], outs[1:]
        groups = [[ins.pop(0) for _ in b] for b in blocks]
        outs = list(outs)
        for i in finish or range(4):
            here = pl.ds(pl.multiple_of(table_ref[8 + i] * row, row), row)
            left, right = [], []
            for slot, group in zip(slots, groups):
                cols = pl.ds(pl.multiple_of(table_ref[slot] * depth, depth), depth)
                left += [a_ref[t, here, cols] for t in range(tiles)]
                sides = [r[:, :, lo:hi] if len(group) == 1 and r.shape[2] > columns else r[...] for r in group]
                block = sides[0] if len(sides) == 1 else jnp.concatenate(sides, axis=2)
                right.append(block.reshape(tiles * depth, columns))
            acc = jnp.dot(
                jnp.concatenate(left, axis=1), jnp.concatenate(right, axis=0), preferred_element_type=F32
            )
            if total is not None:
                acc += total_ref[i, :, lo:hi] if total.shape[2] > columns else total_ref[i]
            if not finish:
                outs[0][i] = acc
            else:
                for n in range(pieces[i]):
                    ref = outs.pop(0)
                    ref[...] = acc[n * ref.shape[0] : (n + 1) * ref.shape[0]].astype(ref.dtype)

    vmem = pl.BlockSpec(memory_space=pltpu.VMEM)
    smem = pl.BlockSpec(memory_space=pltpu.SMEM)
    operands = [a] + flat + ([] if total is None else [total])
    if finish:
        types = (BF16, BF16, F32, F32)
        out_shape = [
            jax.ShapeDtypeStruct((row // pieces[i], columns), types[i]) for i in finish for _ in range(pieces[i])
        ]
    else:
        out_shape = [jax.ShapeDtypeStruct((4, row, columns), F32)]
    out = pl.pallas_call(
        body,
        in_specs=[smem] + [vmem] * len(operands),
        out_specs=[vmem] * len(out_shape),
        out_shape=out_shape,
        compiler_params=pltpu.CompilerParams(vmem_limit_bytes=20 * 2**20),
        cost_estimate=pl.CostEstimate(
            flops=weight * 2 * row * len(finish or range(4)) * tiles * depth * len(blocks) * columns,
            bytes_accessed=min(weight, 1) * (2 * a.size + 2 * len(flat) * tiles * depth * columns),
            transcendentals=0,
        ),
    )(table, *operands)
    return out if finish else out[0]


def device_table():
    even, odd = dict(EVEN), dict(ODD)
    places = []
    for p in range(8):
        slots = [p, even[p], odd[p], odd[even[p]], even[odd[p]], even[odd[even[p]]], odd[even[odd[p]]]]
        places.append(slots + [sum(range(8)) - sum(slots)])
    every = [places[p] + [v ^ s for s in (3, 1, 2, 0)] for p in range(8) for v in range(4)]
    me = lax.axis_index(("pair", "virt"))
    return lax.dynamic_index_in_dim(jnp.array(every, jnp.int32), me, keepdims=False)


def scheduled(amplitudes, tile_mask, integrals, pair_energy, virt_energy):
    table = device_table()
    columns = integrals.shape[2]
    span_a, span_b = (0, columns // 2), (columns // 2, columns)

    def part(v, span):
        return v[:, :, span[0] : span[1]]

    e1 = over_pair(integrals, EVEN)
    own_a, own_b = halves(integrals)
    o1a, o1b = over_pair(own_a, ODD), over_pair(own_b, ODD)
    a = arranged(amplitudes, tile_mask)
    o1a, a, table = tie(o1a, a, table)
    e2a, o2a = over_pair(o1a, EVEN), over_pair(part(e1, span_a), ODD)
    e2b, o2b = over_pair(o1b, EVEN), over_pair(part(e1, span_b), ODD)
    total = products(table, [0, 1, 2], a, [integrals, e1, [o1a, o1b]], (0, columns))
    o2a, e2a, total = tie(o2a, e2a, total)
    e3a, o3a = over_pair(o2a, EVEN), over_pair(e2a, ODD)
    e3b, o3b = over_pair(o2b, EVEN), over_pair(e2b, ODD)
    total = products(table, [3, 4], a, [[e2a, e2b], [o2a, o2b]], (0, columns), total=total)
    e3a, o3a, total = tie(e3a, o3a, total)
    last_a = over_pair(o3a, EVEN)
    total_a = products(table, [5, 6], a, [e3a, o3a], span_a, total=total, weight=20)
    e3b, total_a = tie(e3b, total_a)
    last_b = over_pair(e3b, ODD)

    there_a = products(table, [7], a, [last_a], span_a, total=total_a, finish=(0,), weight=0)
    got_there_a = [over_virt(v, CORE) for v in there_a]
    here_a, keep_there_a, keep_here_a = products(
        table, [7], a, [last_a], span_a, total=total_a, finish=(1, 2, 3), weight=0
    )
    mine_a = added(keep_there_a, got_there_a)
    total, mine_a = tie(total, mine_a)
    total_b = products(table, [5, 6], a, [e3b, o3b], span_b, total=total)
    there_b = products(table, [7], a, [last_b], span_b, total=total_b, finish=(0,), weight=20)
    from_y_a = over_virt(mine_a, YHOP)
    got_there_b = [over_virt(v, CORE) for v in there_b]
    here_b, keep_there_b, keep_here_b = products(
        table, [7], a, [last_b], span_b, total=total_b, finish=(1, 2, 3), weight=0
    )
    from_y_b = over_virt(added(keep_there_b, got_there_b), YHOP)
    got_here_a, got_here_b = over_virt(here_a, CORE), over_virt(here_b, CORE)
    left, inverse = first_quotient(keep_here_a, got_here_a, from_y_a, pair_energy, virt_energy, span_a)
    from_y_b, left = tie(from_y_b, left)
    return second_quotient(keep_here_b, got_here_b, from_y_b, inverse, left)


def solution(mesh):
    placed = (
        P("pair", "virt", None),
        P("pair", "virt"),
        P("virt", "pair", None),
        P(("pair", "virt")),
        P(),
    )
    here = mesh.shape["pair"] == 8 and mesh.shape["virt"] == 4
    return jax.shard_map(
        scheduled if here else plain,
        mesh=mesh,
        in_specs=placed,
        out_specs=P(("pair", "virt"), None),
        check_vma=False,
    )
```
